32 devices in a mesh: groups: 2 (over y), sol: 4 (over z), head: 2 (over x), sub: 2 (over core).
Axes of the slice: x: 2, y: 2, z: 4, core: 2. Of those that a mesh axis runs over, the one named last changes fastest.
Arguments:
- query_key: bfloat16 [16, 512, 2, 2048], P(('groups', 'sol'), None, None, ('head', 'sub')), parts along dimension 0, may hold values from -6 to 6
- values_in: bfloat16 [16, 512, 4096], P(('groups', 'sol'), None, ('head', 'sub')), parts along dimension 0, may hold values from -6 to 6
- gate_in: bfloat16 [16, 512, 4096], P(('groups', 'sol'), None, ('head', 'sub')), parts along dimension 0, may hold values from -6 to 6
- decay_in: float32 [16, 32, 512], P(('groups', 'sol'), ('head', 'sub')), parts along dimension 0, may hold values from -6 to 6
- beta_in: float32 [16, 32, 512], P(('groups', 'sol'), ('head', 'sub')), parts along dimension 0, may hold values from -6 to 6
- decay_rate: float32 [32], P(('head', 'sub')), may hold values from 0.002 to 0.08
- decay_bias: float32 [32], P(('head', 'sub')), may hold values from -1 to 1
- conv_qk: float32 [4, 2, 2048], P(None, None, ('head', 'sub')), may hold values from -3 to 3
- conv_v: float32 [4, 4096], P(None, ('head', 'sub')), may hold values from -3 to 3
- prompt_states: bfloat16 [8, 32, 128, 128], P(('groups', 'sol'), ('head', 'sub')), parts along dimension 0, may hold values from -6 to 6
- prompt_of: int32 [16], P(('groups', 'sol')), parts along dimension 0, may hold values from 0 to 3
- step_ends: int32 [16, 2], P(('groups', 'sol')), parts along dimension 0, may hold values from 1 to 512, as said below
- norm_gain: float32 [128], replicated, may hold values from 0.25 to 1.75
- probe: bfloat16 [4096], replicated, may hold values from -0.09375 to 0.09375
Outputs:
- hidden: bfloat16 [16, 512, 4096], P(('groups', 'sol'), ('head', 'sub')), parts along dimension 0
- step_logits: float32 [16, 2], P(('groups', 'sol')), parts along dimension 0
The draws below stay inside these ranges and needn't reach their ends.
There are 2 independent parts, one for each index of `groups`. The reference program is written for one: setup_inputs(seed, part) draws one part's arguments, and reference() takes and returns one part's arrays. A program takes and returns all parts, laid end to end along the dimension named above; an argument that names none is the same for every part. Nothing has to cross between parts.
Inputs may be any that keep to these rules, and one draw needn't show every extreme that they name: Solution s continues prompt prompt_of[s]. step_ends[s,0] < step_ends[s,1]; the first step covers positions below step_ends[s,0], the second the positions from there below step_ends[s,1]; later positions are padding. Some solution has step_ends[s,1] = 512.
All inputs are finite; a program needn't handle non-finite values.
Results may differ from the reference program's by a relative error of at most 0.0032.
Values may be sent and summed in bfloat16 or wider, within the bound.
A program may use at most 128 MiB of HBM per device.

```python
import math
import jax
import jax.numpy as jnp
from jax import lax

KH = 16
VH = 32
HD = 128
CONV = 4
LEN = 512
SOLS = 8
PROMPTS = 4
KD = 2048
VD = 4096


def draw_step_ends(key, part):
    first_key, second_key = jax.random.split(jax.random.fold_in(key, 7))
    second = jax.random.randint(second_key, (SOLS,), LEN // 2, LEN + 1)
    second = jnp.where(jnp.arange(SOLS) == 0, LEN, second)
    first = jax.random.randint(first_key, (SOLS,), 1, second)
    return jnp.stack([first, second], axis=1).astype(jnp.int32)


def place_ends(entries, key, smallest, top_value):
    extent = entries.shape
    spot = [jax.random.randint(jax.random.fold_in(key, axis), (), 0, extent[axis]) for axis in range(len(extent))]
    entries = entries.at[tuple(spot)].set(smallest)
    longest = extent.index(max(extent))
    spot[longest] = (spot[longest] + 1) % extent[longest]
    return entries.at[tuple(spot)].set(top_value)


def level_of(stream_key, extent, pieces, low, high):
    def one(dim, shards_of):
        heights = jax.random.uniform(jax.random.fold_in(jax.random.fold_in(stream_key, 6), dim), (shards_of,), jnp.float32, low / len(pieces), high / len(pieces))
        return jnp.repeat(jnp.exp(heights), extent[dim] // shards_of).reshape((-1,) + (1,) * (len(extent) - dim - 1))

    gain = one(*pieces[0])
    for cut in pieces[1:]:
        gain = gain * one(*cut)
    return gain


def bell_draw(own_key, shape, scale, bound, cuts=(), held_as=jnp.bfloat16):
    values = scale * jax.random.normal(own_key, shape, jnp.float32)
    if cuts:
        values = values * level_of(own_key, shape, cuts, -0.22, 0.18)
    return jnp.clip(values, -bound, bound).astype(held_as)


def setup_inputs(seed: int = 0, part: int = 0) -> dict:
    arg_keys = jax.random.split(jax.random.key(seed), 15)
    own_keys = jax.random.split(jax.random.fold_in(arg_keys[14], part), 15)
    return {
        "query_key": bell_draw(own_keys[0], (SOLS, LEN, 2, KD), 1.0, 6.0, ((0, 4), (3, 4))),
        "values_in": bell_draw(own_keys[1], (SOLS, LEN, VD), 1.0, 6.0, ((0, 4), (2, 4))),
        "gate_in": bell_draw(own_keys[2], (SOLS, LEN, VD), 1.0, 6.0, ((0, 4), (2, 4))),
        "decay_in": bell_draw(own_keys[3], (SOLS, VH, LEN), 1.0, 6.0, ((0, 4), (1, 4)), jnp.float32),
        "beta_in": bell_draw(own_keys[4], (SOLS, VH, LEN), 1.5, 6.0, ((0, 4), (1, 4)), jnp.float32),
        "decay_rate": jnp.clip(jnp.exp(math.log(0.08) - 3.6888794 * jax.random.uniform(arg_keys[5], (VH,), jnp.float32) ** level_of(arg_keys[5], (VH,), ((0, 4),), -0.2, 0.2)), 0.002, 0.08),
        "decay_bias": jnp.clip(jax.random.uniform(arg_keys[6], (VH,), jnp.float32, -1.0, 1.0) * level_of(arg_keys[6], (VH,), ((0, 4),), -0.4, 0.0), -1.0, 1.0),
        "conv_qk": bell_draw(arg_keys[7], (CONV, 2, KD), CONV ** -0.5, 3.0, ((2, 4),), jnp.float32),
        "conv_v": bell_draw(arg_keys[8], (CONV, VD), CONV ** -0.5, 3.0, ((1, 4),), jnp.float32),
        "prompt_states": bell_draw(own_keys[9], (PROMPTS, VH, HD, HD), 1.0, 6.0, ((0, 4), (1, 4))),
        "prompt_of": place_ends(jax.random.randint(own_keys[10], (SOLS,), 0, PROMPTS), jax.random.fold_in(own_keys[10], 1), 0, PROMPTS - 1).astype(jnp.int32),
        "step_ends": draw_step_ends(jax.random.fold_in(jax.random.fold_in(arg_keys[14], part), 71), part),
        "norm_gain": jnp.clip(1.0 + 0.15 * jax.random.normal(arg_keys[12], (HD,), jnp.float32), 0.25, 1.75),
        "probe": bell_draw(arg_keys[13], (VD,), VD ** -0.5, 0.09375),
    }


def conv_silu(inputs, kernel):
    width = kernel.shape[0]
    count = inputs.shape[1]
    padded = jnp.pad(inputs, ((0, 0), (width - 1, 0), (0, 0)))
    total = jnp.zeros(inputs.shape, jnp.float32)
    for offset in range(width):
        total = total + padded[:, offset:offset + count, :] * kernel[offset]
    return jax.nn.silu(total)

def unit_rows(field, head_size):
    shape = field.shape
    split = field.reshape(shape[:-1] + (shape[-1] // head_size, head_size))
    return split / jnp.sqrt(lax.optimization_barrier(jnp.sum(split * split, axis=-1, keepdims=True)) + 1e-06)

def reference(query_key, values_in, gate_in, decay_in, beta_in, decay_rate, decay_bias, conv_qk, conv_v, prompt_states, prompt_of, step_ends, norm_gain, probe):
    sols = query_key.shape[0]
    mixed = conv_silu(query_key.reshape(sols, LEN, 2 * KD), conv_qk.reshape(CONV, 2 * KD))
    queries = unit_rows(mixed[:, :, :KD], HD) * HD ** (-0.5)
    keys = unit_rows(mixed[:, :, KD:], HD)
    queries = jnp.repeat(queries, VH // KH, axis=2)
    keys = jnp.repeat(keys, VH // KH, axis=2)
    values = conv_silu(values_in, conv_v).reshape(sols, LEN, VH, HD)
    log_decay = -decay_rate[None, :, None] * jax.nn.softplus(decay_in + decay_bias[None, :, None])
    beta = jax.nn.sigmoid(beta_in)
    initial = prompt_states[prompt_of].astype(jnp.float32)
    highest = lax.Precision.HIGHEST

    def advance(state, inputs):
        query, key, value, decay, rate = inputs
        state = jnp.exp(decay)[..., None, None] * state
        guess = jnp.einsum('shkv,shk->shv', state, key, precision=highest)
        state = state + jnp.einsum('shk,shv->shkv', key, rate[..., None] * (value - guess), precision=highest)
        output = jnp.einsum('shkv,shk->shv', state, query, precision=highest)
        return (state, output)
    inputs = (jnp.moveaxis(queries, 1, 0), jnp.moveaxis(keys, 1, 0), jnp.moveaxis(values, 1, 0), jnp.moveaxis(log_decay, 2, 0), jnp.moveaxis(beta, 2, 0))
    unused, outputs = lax.scan(advance, initial, inputs)
    core = jnp.moveaxis(outputs, 0, 1)
    scale = jnp.sqrt(lax.optimization_barrier(jnp.mean(core * core, axis=-1, keepdims=True)) + 1e-06)
    normed = core / scale * norm_gain * jax.nn.silu(gate_in.reshape(sols, LEN, VH, HD).astype(jnp.float32))
    places = jnp.arange(LEN, dtype=jnp.int32)
    live = places[None, :] < step_ends[:, 1:2]
    hidden = jnp.where(live[:, :, None], normed.reshape(sols, LEN, VD), 0.0).astype(jnp.bfloat16)
    reward = jnp.dot(hidden.reshape(sols * LEN, VD), probe, preferred_element_type=jnp.float32).reshape(sols, LEN)
    step_logits = jnp.take_along_axis(reward, (step_ends - 1).astype(jnp.int32), axis=1)
    return (hidden, step_logits)
```

```python
import functools

import jax
import jax.numpy as jnp
from jax import lax
from jax.experimental import pallas as pl
from jax.experimental.pallas import tpu as pltpu
from jax.sharding import PartitionSpec as P

C = 128
F32 = jnp.float32
BF16 = jnp.bfloat16


def dot(a, b):
    return lax.dot_general(a, b, (((1,), (0,)), ((), ())), preferred_element_type=F32)


def split(x):
    high = x.astype(BF16)
    return high, (x - high.astype(F32)).astype(BF16)


def pack(x):
    return jnp.concatenate(split(x), axis=1)


def pack_right(x):
    row = pack(x)
    return jnp.concatenate([row, row], axis=0)


def packed_dot(left, right):
    both = dot(left, right)
    return both[:, :C] + both[:, C:]


def silu(x):
    return x / (1.0 + jnp.exp(-x))


def conv_silu(x, taps):
    rows = lax.broadcasted_iota(jnp.int32, x.shape, 0)
    total = x * taps[3:4]
    for back in range(1, 4):
        moved = jnp.where(rows >= back, pltpu.roll(x, back, 0), 0.0)
        total = total + moved * taps[3 - back : 4 - back]
    return silu(total)


def unit(x):
    return x * lax.rsqrt(jnp.sum(x * x, axis=-1, keepdims=True) + 1e-06)


def kernel(
    ends_ref, owner_ref, qk_ref, v_ref, gate_ref, decay_ref, beta_ref, rate_ref, bias_ref, tqk_ref, tv_ref,
    init_ref, gain_ref, hid_ref, sel_ref, rows_ref, kq_ref, kt_ref, x_ref, score_ref, vb_ref, s_ref,
):
    sols, length, width = v_ref.shape
    heads = width // C
    groups = heads // 2
    count = length // C
    ii = lax.broadcasted_iota(jnp.int32, (C, C), 0)
    jj = lax.broadcasted_iota(jnp.int32, (C, C), 1)
    ones = jnp.where(ii <= jj, 1.0, 0.0).astype(F32)

    def one_solution(s, carry):
        log_decay = -rate_ref[...] * jax.nn.softplus(decay_ref[s] + bias_ref[...])
        beta = jax.nn.sigmoid(beta_ref[s])
        for c in range(count):
            cols = slice(c * C, (c + 1) * C)
            cum = lax.dot_general(
                log_decay[:, cols], ones, (((1,), (0,)), ((), ())),
                precision=lax.Precision.HIGHEST, preferred_element_type=F32,
            )
            for g in range(groups):
                pair = slice(2 * g, 2 * g + 2)
                rows_ref[g, c] = jnp.concatenate(
                    [cum[pair], beta[pair, cols], jnp.zeros((4, C), F32)], axis=0
                )

        def prepare(g, carry):
            at = pl.ds(pl.multiple_of(g * C, C), C)
            at2 = pl.ds(pl.multiple_of(width // 2 + g * C, C), C)
            q = unit(conv_silu(qk_ref[s, :, at].astype(F32), tqk_ref[:, at])) * C ** (-0.5)
            k = unit(conv_silu(qk_ref[s, :, at2].astype(F32), tqk_ref[:, at2]))
            atv = pl.ds(pl.multiple_of(g * 2 * C, 2 * C), 2 * C)
            v = conv_silu(v_ref[s, :, atv].astype(F32), tv_ref[:, atv])
            systems = []
            for c in range(count):
                span = slice(c * C, (c + 1) * C)
                kt = jnp.transpose(k[span])
                kth, ktl = split(kt)
                ktp = jnp.concatenate([kth, ktl], axis=1)
                kt_ref[g, c] = ktp
                kqp = jnp.concatenate([pack(k[span]), pack(q[span])], axis=0)
                kq_ref[g, c] = kqp
                gram = packed_dot(kqp, jnp.concatenate([ktp, ktp], axis=0))
                rows = rows_ref[g, c]
                cols = jnp.transpose(rows)
                for h in range(2):
                    spread = cols[:, h : h + 1] - rows[h : h + 1, :]
                    weights = jnp.exp(jnp.where(ii >= jj, spread, -1e30))
                    rate = cols[:, 2 + h : 3 + h]
                    score_ref[g, c, h] = pack(gram[C:] * weights)
                    systems.append(jnp.where(ii > jj, rate * gram[:C] * weights, 0.0))
                    vb_ref[g, c, :, h * C : (h + 1) * C] = rate * v[span, h * C : (h + 1) * C]
            far = ii ^ jj
            eye = jnp.where(ii == jj, 1.0, 0.0)
            inverses = [eye - jnp.where(far == 1, m, 0.0) for m in systems]
            b = 2
            while b < C:
                near = (far >= b) & (far < 2 * b)
                packs = [pack(x) for x in inverses]
                mids = [
                    packed_dot(p, pack_right(jnp.where(near, m, 0.0)))
                    for p, m in zip(packs, systems)
                ]
                inverses = [
                    x - packed_dot(pack(y), jnp.concatenate([p, p], axis=0))
                    for x, y, p in zip(inverses, mids, packs)
                ]
                b *= 2
            for c in range(count):
                for h in range(2):
                    x_ref[g, c, h] = pack(inverses[2 * c + h])
            return carry

        lax.fori_loop(0, groups, prepare, 0)

        for g in range(groups):
            for h in range(2):
                s_ref[g, :, h * C : (h + 1) * C] = init_ref[owner_ref[s], 2 * g + h].astype(F32)

        def advance(c, carry):
            span = pl.ds(pl.multiple_of(c * C, C), C)
            place = c * C + lax.broadcasted_iota(jnp.int32, (C, 1), 0)
            live = place < ends_ref[s, 1]
            row = lax.broadcasted_iota(jnp.int32, (8, C), 0)
            lane = c * C + lax.broadcasted_iota(jnp.int32, (8, C), 1)
            pick = jnp.where(
                ((row == 0) & (lane == ends_ref[s, 0] - 1)) | ((row == 1) & (lane == ends_ref[s, 1] - 1)),
                1.0, 0.0,
            ).astype(BF16)
            for g in range(groups):
                state = s_ref[g]
                sh, sl = split(state)
                kqp = kq_ref[g, c]
                reads = dot(kqp, jnp.concatenate([sh, sh], axis=0)) + dot(kqp[:, :C], sl)
                rows = rows_ref[g, c]
                cols = jnp.transpose(rows)
                tails, keeps = [], []
                for h in range(2):
                    part = slice(h * C, (h + 1) * C)
                    cum = cols[:, h : h + 1]
                    grown = jnp.exp(cum)
                    last = rows[h : h + 1, C - 1 : C]
                    right = vb_ref[g, c, :, part] - (cols[:, 2 + h : 3 + h] * grown) * reads[:C, part]
                    fresh = packed_dot(x_ref[g, c, h], pack_right(right))
                    core = grown * reads[C:, part] + packed_dot(score_ref[g, c, h], pack_right(fresh))
                    tails.append(fresh * jnp.exp(last - cum))
                    keeps.append(jnp.exp(last) * state[:, part])
                    scale = lax.rsqrt(jnp.mean(core * core, axis=-1, keepdims=True) + 1e-06)
                    chan = pl.ds((2 * g + h) * C, C)
                    gate = gate_ref[s, span, chan].astype(F32)
                    out = core * scale * gain_ref[...] * silu(gate)
                    hid = jnp.where(live, out, 0.0).astype(BF16)
                    share = length // hid_ref.shape[0]
                    for d in range(C // share):
                        hid_ref[c * (C // share) + d, s, :, chan] = hid[d * share : (d + 1) * share]
                    chosen = dot(pick, hid)
                    old = jnp.where(c == 0, 0.0, sel_ref[s, :, chan])
                    sel_ref[s, :, chan] = old + chosen
                fresh = jnp.concatenate(tails, axis=1)
                fh, fl = split(fresh)
                ktp = kt_ref[g, c]
                s_ref[g] = (
                    jnp.concatenate(keeps, axis=1)
                    + dot(ktp, jnp.concatenate([fh, fh], axis=0))
                    + dot(ktp[:, :C], fl)
                )
            return carry

        lax.fori_loop(0, count, advance, 0)
        return carry

    lax.fori_loop(0, sols, one_solution, 0)


def run_layer(ends, owner, qk, v, gate, decay, beta, rate, bias, tqk, tv, init, gain):
    sols, length, width = v.shape
    groups = width // C // 2
    count = length // C
    shares = lax.axis_size(("head", "sub"))
    vmem = pl.BlockSpec(memory_space=pltpu.VMEM)
    return pl.pallas_call(
        kernel,
        out_shape=(
            jax.ShapeDtypeStruct((shares, sols, length // shares, width), BF16),
            jax.ShapeDtypeStruct((sols, 8, width), F32),
        ),
        in_specs=[pl.BlockSpec(memory_space=pltpu.SMEM)] * 2 + [vmem] * 11,
        out_specs=(vmem, vmem),
        scratch_shapes=[
            pltpu.VMEM((groups, count, 8, C), F32),
            pltpu.VMEM((groups, count, 2 * C, 2 * C), BF16),
            pltpu.VMEM((groups, count, C, 2 * C), BF16),
            pltpu.VMEM((groups, count, 2, C, 2 * C), BF16),
            pltpu.VMEM((groups, count, 2, C, 2 * C), BF16),
            pltpu.VMEM((groups, count, C, 2 * C), F32),
            pltpu.VMEM((groups, C, 2 * C), F32),
        ],
        compiler_params=pltpu.CompilerParams(vmem_limit_bytes=56 * 1024 * 1024),
        name="delta_layer",
    )(ends, owner, qk, v, gate, decay, beta, rate, bias, tqk, tv, init, gain)


def on_device(
    query_key, values_in, gate_in, decay_in, beta_in, decay_rate, decay_bias, conv_qk, conv_v,
    prompt_states, prompt_of, step_ends, norm_gain, probe,
):
    sols, length, _, key_width = query_key.shape
    width = values_in.shape[2]
    every = lax.all_gather(prompt_states, "sol", axis=0, tiled=True)
    hidden, chosen = run_layer(
        step_ends, prompt_of,
        query_key.reshape(sols, length, 2 * key_width),
        values_in, gate_in, decay_in, beta_in, decay_rate[:, None], decay_bias[:, None],
        conv_qk.reshape(conv_qk.shape[0], 2 * key_width), conv_v, every, norm_gain[None, :],
    )
    me = lax.axis_index(("head", "sub"))
    part = lax.dynamic_slice_in_dim(probe, me * width, width, 0).astype(F32)
    logits = lax.psum(jnp.sum(chosen[:, :2] * part, axis=-1), ("head", "sub"))
    moved = lax.all_to_all(hidden, ("head", "sub"), split_axis=0, concat_axis=0, tiled=True)
    share = length // hidden.shape[0]
    return moved.transpose(1, 2, 0, 3).reshape(sols, share, hidden.shape[0] * width), logits


def solution(mesh):
    return jax.shard_map(
        on_device,
        mesh=mesh,
        in_specs=(
            P(("groups", "sol"), None, None, ("head", "sub")),
            P(("groups", "sol"), None, ("head", "sub")),
            P(("groups", "sol"), None, ("head", "sub")),
            P(("groups", "sol"), ("head", "sub"), None),
            P(("groups", "sol"), ("head", "sub"), None),
            P(("head", "sub")),
            P(("head", "sub")),
            P(None, None, ("head", "sub")),
            P(None, ("head", "sub")),
            P(("groups", "sol"), ("head", "sub"), None, None),
            P(("groups", "sol")),
            P(("groups", "sol"), None),
            P(),
            P(),
        ),
        out_specs=(P(("groups", "sol"), ("head", "sub"), None), P(("groups", "sol"), None)),
        check_vma=False,
    )
```

```python
import jax
import jax.numpy as jnp
from jax import lax
from jax.experimental import pallas as pl
from jax.experimental.pallas import tpu as pltpu
from jax.sharding import PartitionSpec as P

C = 128
F32 = jnp.float32
BF16 = jnp.bfloat16
MESH = pl.DeviceIdType.MESH


def dot(a, b):
    return lax.dot_general(a, b, (((1,), (0,)), ((), ())), preferred_element_type=F32)


def split(x):
    high = x.astype(BF16)
    return high, (x - high.astype(F32)).astype(BF16)


def pack(x):
    return jnp.concatenate(split(x), axis=1)


def pack_right(x):
    row = pack(x)
    return jnp.concatenate([row, row], axis=0)


def packed_dot(left, right):
    both = dot(left, right)
    return both[:, :C] + both[:, C:]


def silu(x):
    return x / (1.0 + jnp.exp(-x))


def conv_silu(x, taps):
    rows = lax.broadcasted_iota(jnp.int32, x.shape, 0)
    total = x * taps[3:4]
    for back in range(1, 4):
        moved = jnp.where(rows >= back, pltpu.roll(x, back, 0), 0.0)
        total = total + moved * taps[3 - back : 4 - back]
    return silu(total)


def unit(x):
    return x * lax.rsqrt(jnp.sum(x * x, axis=-1, keepdims=True) + 1e-06)


def kernel(
    ends_ref, owner_ref, qk_ref, v_ref, gate_ref, decay_ref, beta_ref, rate_ref, bias_ref, tqk_ref, tv_ref,
    own_ref, gain_ref, probe_ref, out_ref, logit_ref, hid_ref, sel_ref, rows_ref, kq_ref, kt_ref, x_ref,
    score_ref, vb_ref, s_ref, every_ref, part_ref, st_send, st_recv, hid_send, hid_recv, lg_send, lg_recv, local_sem,
):
    sols, length, width = v_ref.shape
    n_sol, n_sub = lax.axis_size("sol"), lax.axis_size("sub")
    shares = lax.axis_size("head") * n_sub
    share = length // shares
    per_chunk = C // share
    prompts = own_ref.shape[0]
    my_sol = lax.axis_index("sol")
    me = lax.axis_index("head") * n_sub + lax.axis_index("sub")

    def mate(index):
        return {"head": index // n_sub, "sub": index % n_sub}

    barrier = pltpu.get_barrier_semaphore()
    for r in range(1, n_sol):
        pl.semaphore_signal(barrier, 1, device_id={"sol": lax.rem(my_sol + r, n_sol)}, device_id_type=MESH)
    for r in range(1, shares):
        pl.semaphore_signal(barrier, 1, device_id=mate(lax.rem(me + r, shares)), device_id_type=MESH)
    pl.semaphore_wait(barrier, n_sol + shares - 2)

    def state_copy(r, slot):
        return pltpu.make_async_remote_copy(
            src_ref=own_ref, dst_ref=every_ref.at[pl.ds(slot * prompts, prompts)],
            send_sem=st_send.at[r - 1], recv_sem=st_recv.at[r - 1],
            device_id={"sol": lax.rem(my_sol + r, n_sol)}, device_id_type=MESH,
        )

    def hidden_copy(s, to, source):
        return pltpu.make_async_remote_copy(
            src_ref=hid_ref.at[to, s],
            dst_ref=out_ref.at[s, :, pl.ds(pl.multiple_of(source * width, width), width)],
            send_sem=hid_send.at[s, to], recv_sem=hid_recv.at[s, source],
            device_id=mate(to), device_id_type=MESH,
        )

    def hidden_local(s):
        return pltpu.make_async_copy(
            hid_ref.at[me, s], out_ref.at[s, :, pl.ds(pl.multiple_of(me * width, width), width)],
            local_sem.at[s],
        )

    def part_copy(r, slot):
        return pltpu.make_async_remote_copy(
            src_ref=part_ref.at[slot], dst_ref=part_ref.at[slot],
            send_sem=lg_send.at[r - 1], recv_sem=lg_recv.at[r - 1],
            device_id=mate(lax.rem(me + r, shares)), device_id_type=MESH,
        )

    for r in range(1, n_sol):
        state_copy(r, my_sol).start()
    every_ref[pl.ds(my_sol * prompts, prompts)] = own_ref[...]
    heads = width // C
    groups = heads // 2
    count = length // C
    ii = lax.broadcasted_iota(jnp.int32, (C, C), 0)
    jj = lax.broadcasted_iota(jnp.int32, (C, C), 1)
    ones = jnp.where(ii <= jj, 1.0, 0.0).astype(F32)

    def one_solution(s, carry):
        log_decay = -rate_ref[...] * jax.nn.softplus(decay_ref[s] + bias_ref[...])
        beta = jax.nn.sigmoid(beta_ref[s])
        for c in range(count):
            cols = slice(c * C, (c + 1) * C)
            cum = lax.dot_general(
                log_decay[:, cols], ones, (((1,), (0,)), ((), ())),
                precision=lax.Precision.HIGHEST, preferred_element_type=F32,
            )
            for g in range(groups):
                pair = slice(2 * g, 2 * g + 2)
                rows_ref[g, c] = jnp.concatenate(
                    [cum[pair], beta[pair, cols], jnp.zeros((4, C), F32)], axis=0
                )

        def prepare(g, carry):
            at = pl.ds(pl.multiple_of(g * C, C), C)
            at2 = pl.ds(pl.multiple_of(width // 2 + g * C, C), C)
            q = unit(conv_silu(qk_ref[s, :, at].astype(F32), tqk_ref[:, at])) * C ** (-0.5)
            k = unit(conv_silu(qk_ref[s, :, at2].astype(F32), tqk_ref[:, at2]))
            atv = pl.ds(pl.multiple_of(g * 2 * C, 2 * C), 2 * C)
            v = conv_silu(v_ref[s, :, atv].astype(F32), tv_ref[:, atv])
            systems = []
            for c in range(count):
                span = slice(c * C, (c + 1) * C)
                kt = jnp.transpose(k[span])
                kth, ktl = split(kt)
                ktp = jnp.concatenate([kth, ktl], axis=1)
                kt_ref[g, c] = ktp
                kqp = jnp.concatenate([pack(k[span]), pack(q[span])], axis=0)
                kq_ref[g, c] = kqp
                gram = packed_dot(kqp, jnp.concatenate([ktp, ktp], axis=0))
                rows = rows_ref[g, c]
                cols = jnp.transpose(rows)
                for h in range(2):
                    spread = cols[:, h : h + 1] - rows[h : h + 1, :]
                    weights = jnp.exp(jnp.where(ii >= jj, spread, -1e30))
                    rate = cols[:, 2 + h : 3 + h]
                    score_ref[g, c, h] = pack(gram[C:] * weights)
                    systems.append(jnp.where(ii > jj, rate * gram[:C] * weights, 0.0))
                    vb_ref[g, c, :, h * C : (h + 1) * C] = rate * v[span, h * C : (h + 1) * C]
            far = ii ^ jj
            eye = jnp.where(ii == jj, 1.0, 0.0)
            inverses = [eye - jnp.where(far == 1, m, 0.0) for m in systems]
            b = 2
            while b < C:
                near = (far >= b) & (far < 2 * b)
                packs = [pack(x) for x in inverses]
                mids = [
                    packed_dot(p, pack_right(jnp.where(near, m, 0.0)))
                    for p, m in zip(packs, systems)
                ]
                inverses = [
                    x - packed_dot(pack(y), jnp.concatenate([p, p], axis=0))
                    for x, y, p in zip(inverses, mids, packs)
                ]
                b *= 2
            for c in range(count):
                for h in range(2):
                    x_ref[g, c, h] = pack(inverses[2 * c + h])
            return carry

        lax.fori_loop(0, groups, prepare, 0)

        @pl.when(s == 0)
        def _():
            for r in range(1, n_sol):
                state_copy(r, lax.rem(my_sol + n_sol - r, n_sol)).wait_recv()

        for g in range(groups):
            for h in range(2):
                s_ref[g, :, h * C : (h + 1) * C] = every_ref[owner_ref[s], 2 * g + h].astype(F32)

        def advance(c, carry):
            span = pl.ds(pl.multiple_of(c * C, C), C)
            place = c * C + lax.broadcasted_iota(jnp.int32, (C, 1), 0)
            live = place < ends_ref[s, 1]
            row = lax.broadcasted_iota(jnp.int32, (8, C), 0)
            lane = c * C + lax.broadcasted_iota(jnp.int32, (8, C), 1)
            pick = jnp.where(
                ((row == 0) & (lane == ends_ref[s, 0] - 1)) | ((row == 1) & (lane == ends_ref[s, 1] - 1)),
                1.0, 0.0,
            ).astype(BF16)
            for g in range(groups):
                state = s_ref[g]
                sh, sl = split(state)
                kqp = kq_ref[g, c]
                reads = dot(kqp, jnp.concatenate([sh, sh], axis=0)) + dot(kqp[:, :C], sl)
                rows = rows_ref[g, c]
                cols = jnp.transpose(rows)
                tails, keeps = [], []
                for h in range(2):
                    part = slice(h * C, (h + 1) * C)
                    cum = cols[:, h : h + 1]
                    grown = jnp.exp(cum)
                    last = rows[h : h + 1, C - 1 : C]
                    right = vb_ref[g, c, :, part] - (cols[:, 2 + h : 3 + h] * grown) * reads[:C, part]
                    fresh = packed_dot(x_ref[g, c, h], pack_right(right))
                    core = grown * reads[C:, part] + packed_dot(score_ref[g, c, h], pack_right(fresh))
                    tails.append(fresh * jnp.exp(last - cum))
                    keeps.append(jnp.exp(last) * state[:, part])
                    scale = lax.rsqrt(jnp.mean(core * core, axis=-1, keepdims=True) + 1e-06)
                    chan = pl.ds((2 * g + h) * C, C)
                    gate = gate_ref[s, span, chan].astype(F32)
                    out = core * scale * gain_ref[...] * silu(gate)
                    hid = jnp.where(live, out, 0.0).astype(BF16)
                    for d in range(per_chunk):
                        hid_ref[c * per_chunk + d, s, :, chan] = hid[d * share : (d + 1) * share]
                    chosen = dot(pick, hid)
                    old = jnp.where(c == 0, 0.0, sel_ref[s, :, chan])
                    sel_ref[s, :, chan] = old + chosen
                fresh = jnp.concatenate(tails, axis=1)
                fh, fl = split(fresh)
                ktp = kt_ref[g, c]
                s_ref[g] = (
                    jnp.concatenate(keeps, axis=1)
                    + dot(ktp, jnp.concatenate([fh, fh], axis=0))
                    + dot(ktp[:, :C], fl)
                )
            for d in range(per_chunk):
                to = c * per_chunk + d

                @pl.when(to == me)
                def _():
                    hidden_local(s).start()

                @pl.when(to != me)
                def _():
                    hidden_copy(s, to, me).start()

            return carry

        lax.fori_loop(0, count, advance, 0)
        logit = jnp.sum(sel_ref[s] * probe_ref[me], axis=-1, keepdims=True)
        part_ref[me, s] = jnp.broadcast_to(logit, (8, C))
        return carry

    lax.fori_loop(0, sols, one_solution, 0)

    for r in range(1, shares):
        part_copy(r, me).start()
    for r in range(1, shares):
        part_copy(r, me).wait_send()
        part_copy(r, lax.rem(me + shares - r, shares)).wait_recv()
    total = part_ref[0]
    for other in range(1, shares):
        total = total + part_ref[other]
    logit_ref[...] = total
    for r in range(1, n_sol):
        state_copy(r, my_sol).wait_send()
    for s in range(sols):
        hidden_local(s).wait()
        for r in range(1, shares):
            hidden_copy(s, lax.rem(me + r, shares), me).wait_send()
            other = lax.rem(me + shares - r, shares)
            hidden_copy(s, other, other).wait_recv()


def run_layer(ends, owner, qk, v, gate, decay, beta, rate, bias, tqk, tv, own, gain, probe):
    sols, length, width = v.shape
    groups = width // C // 2
    count = length // C
    shares = lax.axis_size(("head", "sub"))
    n_sol = lax.axis_size("sol")
    vmem = pl.BlockSpec(memory_space=pltpu.VMEM)
    return pl.pallas_call(
        kernel,
        out_shape=(
            jax.ShapeDtypeStruct((sols, length // shares, shares * width), BF16),
            jax.ShapeDtypeStruct((sols, 8, C), F32),
        ),
        in_specs=[pl.BlockSpec(memory_space=pltpu.SMEM)] * 2 + [vmem] * 12,
        out_specs=(pl.BlockSpec(memory_space=pl.ANY), vmem),
        scratch_shapes=[
            pltpu.VMEM((shares, sols, length // shares, width), BF16),
            pltpu.VMEM((sols, 8, width), F32),
            pltpu.VMEM((groups, count, 8, C), F32),
            pltpu.VMEM((groups, count, 2 * C, 2 * C), BF16),
            pltpu.VMEM((groups, count, C, 2 * C), BF16),
            pltpu.VMEM((groups, count, 2, C, 2 * C), BF16),
            pltpu.VMEM((groups, count, 2, C, 2 * C), BF16),
            pltpu.VMEM((groups, count, C, 2 * C), F32),
            pltpu.VMEM((groups, C, 2 * C), F32),
            pltpu.VMEM((n_sol * own.shape[0],) + own.shape[1:], BF16),
            pltpu.VMEM((shares, sols, 8, C), F32),
            pltpu.SemaphoreType.DMA((n_sol - 1,)),
            pltpu.SemaphoreType.DMA((n_sol - 1,)),
            pltpu.SemaphoreType.DMA((sols, shares)),
            pltpu.SemaphoreType.DMA((sols, shares)),
            pltpu.SemaphoreType.DMA((shares - 1,)),
            pltpu.SemaphoreType.DMA((shares - 1,)),
            pltpu.SemaphoreType.DMA((sols,)),
        ],
        compiler_params=pltpu.CompilerParams(vmem_limit_bytes=56 * 1024 * 1024, collective_id=0, has_side_effects=True),
        name="delta_layer",
    )(ends, owner, qk, v, gate, decay, beta, rate, bias, tqk, tv, own, gain, probe)


def on_device(
    query_key, values_in, gate_in, decay_in, beta_in, decay_rate, decay_bias, conv_qk, conv_v,
    prompt_states, prompt_of, step_ends, norm_gain, probe,
):
    sols, length, _, key_width = query_key.shape
    width = values_in.shape[2]
    shares = lax.axis_size(("head", "sub"))
    hidden, logits = run_layer(
        step_ends, prompt_of,
        query_key.reshape(sols, length, 2 * key_width),
        values_in, gate_in, decay_in, beta_in, decay_rate[:, None], decay_bias[:, None],
        conv_qk.reshape(conv_qk.shape[0], 2 * key_width), conv_v, prompt_states, norm_gain[None, :],
        probe.astype(F32).reshape(shares, 1, width),
    )
    return hidden, logits[:, :2, 0]


def solution(mesh):
    return jax.shard_map(
        on_device,
        mesh=mesh,
        in_specs=(
            P(("groups", "sol"), None, None, ("head", "sub")),
            P(("groups", "sol"), None, ("head", "sub")),
            P(("groups", "sol"), None, ("head", "sub")),
            P(("groups", "sol"), ("head", "sub"), None),
            P(("groups", "sol"), ("head", "sub"), None),
            P(("head", "sub")),
            P(("head", "sub")),
            P(None, None, ("head", "sub")),
            P(None, ("head", "sub")),
            P(("groups", "sol"), ("head", "sub"), None, None),
            P(("groups", "sol")),
            P(("groups", "sol"), None),
            P(),
            P(),
        ),
        out_specs=(P(("groups", "sol"), ("head", "sub"), None), P(("groups", "sol"), None)),
        check_vma=False,
    )
```

```python
import jax
import jax.numpy as jnp
from jax import lax
from jax.experimental import pallas as pl
from jax.experimental.pallas import tpu as pltpu
from jax.sharding import PartitionSpec as P

C = 128
F32 = jnp.float32
BF16 = jnp.bfloat16
MESH = pl.DeviceIdType.MESH


def dot(a, b):
    return lax.dot_general(a, b, (((1,), (0,)), ((), ())), preferred_element_type=F32)


def split(x):
    high = x.astype(BF16)
    return high, (x - high.astype(F32)).astype(BF16)


def pack(x):
    return jnp.concatenate(split(x), axis=1)


def pack_right(x):
    row = pack(x)
    return jnp.concatenate([row, row], axis=0)


def packed_dot(left, right):
    both = dot(left, right)
    return both[:, :C] + both[:, C:]


def silu(x):
    return x / (1.0 + jnp.exp(-x))


def conv_silu(x, taps):
    rows = lax.broadcasted_iota(jnp.int32, x.shape, 0)
    total = x * taps[3:4]
    for back in range(1, 4):
        moved = jnp.where(rows >= back, pltpu.roll(x, back, 0), 0.0)
        total = total + moved * taps[3 - back : 4 - back]
    return silu(total)


def unit(x):
    return x * lax.rsqrt(jnp.sum(x * x, axis=-1, keepdims=True) + 1e-06)


def kernel(
    ends_ref, owner_ref, qk_ref, v_ref, gate_ref, decay_ref, beta_ref, rate_ref, bias_ref, tqk_ref, tv_ref,
    own_ref, gain_ref, probe_ref, out_ref, logit_ref, hid_ref, sel_ref, rows_ref, kq_ref, kt_ref, x_ref,
    score_ref, vb_ref, s_ref, every_ref, part_ref, mask_ref, st_send, st_recv, hid_send, hid_recv, lg_send, lg_recv, local_sem,
):
    sols, length, width = v_ref.shape
    n_sol, n_sub = lax.axis_size("sol"), lax.axis_size("sub")
    shares = lax.axis_size("head") * n_sub
    share = length // shares
    per_chunk = C // share
    prompts = own_ref.shape[0]
    my_sol = lax.axis_index("sol")
    me = lax.axis_index("head") * n_sub + lax.axis_index("sub")

    def mate(index):
        return {"head": index // n_sub, "sub": index % n_sub}

    barrier = pltpu.get_barrier_semaphore()
    for r in range(1, n_sol):
        pl.semaphore_signal(barrier, 1, device_id={"sol": lax.rem(my_sol + r, n_sol)}, device_id_type=MESH)
    for r in range(1, shares):
        pl.semaphore_signal(barrier, 1, device_id=mate(lax.rem(me + r, shares)), device_id_type=MESH)
    pl.semaphore_wait(barrier, n_sol + shares - 2)

    def state_copy(r, slot):
        return pltpu.make_async_remote_copy(
            src_ref=own_ref, dst_ref=every_ref.at[pl.ds(slot * prompts, prompts)],
            send_sem=st_send.at[r - 1], recv_sem=st_recv.at[r - 1],
            device_id={"sol": lax.rem(my_sol + r, n_sol)}, device_id_type=MESH,
        )

    def hidden_copy(s, to, source):
        return pltpu.make_async_remote_copy(
            src_ref=hid_ref.at[to, s],
            dst_ref=out_ref.at[s, :, pl.ds(pl.multiple_of(source * width, width), width)],
            send_sem=hid_send.at[s, to], recv_sem=hid_recv.at[s, source],
            device_id=mate(to), device_id_type=MESH,
        )

    def hidden_local(s):
        return pltpu.make_async_copy(
            hid_ref.at[me, s], out_ref.at[s, :, pl.ds(pl.multiple_of(me * width, width), width)],
            local_sem.at[s],
        )

    def part_copy(r, slot):
        return pltpu.make_async_remote_copy(
            src_ref=part_ref.at[slot], dst_ref=part_ref.at[slot],
            send_sem=lg_send.at[r - 1], recv_sem=lg_recv.at[r - 1],
            device_id=mate(lax.rem(me + r, shares)), device_id_type=MESH,
        )

    for r in range(1, n_sol):
        state_copy(r, my_sol).start()
    every_ref[pl.ds(my_sol * prompts, prompts)] = own_ref[...]
    heads = width // C
    groups = heads // 2
    count = length // C
    ii = lax.broadcasted_iota(jnp.int32, (C, C), 0)
    jj = lax.broadcasted_iota(jnp.int32, (C, C), 1)
    ones = jnp.where(ii <= jj, 1.0, 0.0).astype(F32)
    far = ii ^ jj
    for at, (least, most) in enumerate(((2, 4), (4, 8), (8, 16), (16, 32), (32, 64), (64, 128), (0, 32), (0, 64))):
        mask = jnp.where((far >= least) & (far < most), 1.0, 0.0).astype(BF16)
        mask_ref[at] = jnp.concatenate([mask, mask], axis=1)
    head = lax.broadcasted_iota(jnp.int32, (heads, 1), 0)
    rate_col = jnp.zeros((heads, 1), F32)
    bias_col = jnp.zeros((heads, 1), F32)
    for h in range(heads):
        rate_col = jnp.where(head == h, rate_ref[h], rate_col)
        bias_col = jnp.where(head == h, bias_ref[h], bias_col)

    def one_solution(s, carry):
        log_decay = -rate_col * jax.nn.softplus(decay_ref[s] + bias_col)
        beta = jax.nn.sigmoid(beta_ref[s])
        for c in range(count):
            cols = slice(c * C, (c + 1) * C)
            cum = lax.dot_general(
                log_decay[:, cols], ones, (((1,), (0,)), ((), ())),
                precision=lax.Precision.HIGHEST, preferred_element_type=F32,
            )
            for g in range(groups):
                pair = slice(2 * g, 2 * g + 2)
                rows_ref[g, c] = jnp.concatenate(
                    [cum[pair], beta[pair, cols], jnp.zeros((4, C), F32)], axis=0
                )

        def prepare(g, carry):
            at = pl.ds(pl.multiple_of(g * C, C), C)
            at2 = pl.ds(pl.multiple_of(width // 2 + g * C, C), C)
            q = unit(conv_silu(qk_ref[s, :, at].astype(F32), tqk_ref[:, 0, at])) * C ** (-0.5)
            k = unit(conv_silu(qk_ref[s, :, at2].astype(F32), tqk_ref[:, 1, at]))
            atv = pl.ds(pl.multiple_of(g * 2 * C, 2 * C), 2 * C)
            v = conv_silu(v_ref[s, :, atv].astype(F32), tv_ref[:, atv])
            systems = []
            for c in range(count):
                span = slice(c * C, (c + 1) * C)
                kt = jnp.transpose(k[span])
                kth, ktl = split(kt)
                ktp = jnp.concatenate([kth, ktl], axis=1)
                kt_ref[g, c] = ktp
                kqp = jnp.concatenate([pack(k[span]), pack(q[span])], axis=0)
                kq_ref[g, c] = kqp
                gram = packed_dot(kqp, jnp.concatenate([ktp, ktp], axis=0))
                rows = rows_ref[g, c]
                cols = jnp.transpose(rows)
                for h in range(2):
                    spread = cols[:, h : h + 1] - rows[h : h + 1, :]
                    weights = jnp.exp(jnp.where(ii >= jj, spread, -1e30))
                    rate = cols[:, 2 + h : 3 + h]
                    score_ref[g, c, h] = pack(gram[C:] * weights)
                    systems.append(jnp.where(ii > jj, rate * gram[:C] * weights, 0.0))
                    vb_ref[g, c, :, h * C : (h + 1) * C] = rate * v[span, h * C : (h + 1) * C]
            parts = [pack(m) for m in systems]
            wide = [jnp.where((ii ^ jj) == 1, m, 0.0) for m in systems]
            eye = jnp.where((ii[:32] ^ (jj[:32] & 31)) == 0, 1.0, 0.0)
            small = [eye - (m[:32] + m[32:64] + m[64:96] + m[96:]) for m in wide]

            def tile(p, at):
                rows = jnp.concatenate([p] * (C // p.shape[0]), axis=0) * mask_ref[at]
                return jnp.concatenate([rows, rows], axis=0)

            def near(p, at):
                rows = p * mask_ref[at]
                return jnp.concatenate([rows, rows], axis=0)

            for level in range(4):
                packs = [pack(x) for x in small]
                mids = [packed_dot(p, near(m, level)) for p, m in zip(packs, parts)]
                small = [x - packed_dot(pack(y), tile(p, 6)) for x, y, p in zip(small, mids, packs)]
            half = lax.broadcasted_iota(jnp.int32, (64, C), 0) ^ lax.broadcasted_iota(jnp.int32, (64, C), 1)
            small = [jnp.where((half & 32) == 0, jnp.concatenate([x, x], axis=0), 0.0) for x in small]
            packs = [pack(x) for x in small]
            mids = [packed_dot(p, near(m, 4)) for p, m in zip(packs, parts)]
            small = [x - packed_dot(pack(y), tile(p, 7)) for x, y, p in zip(small, mids, packs)]
            packs = [pack(x) for x in small]
            fulls = [jnp.concatenate([p, p], axis=0) * mask_ref[7] for p in packs]
            mids = [packed_dot(f[64:], near(m, 5)) for f, m in zip(fulls, parts)]
            lows = [packed_dot(pack(y), jnp.concatenate([f, f], axis=0)) for y, f in zip(mids, fulls)]
            inverses = [
                jnp.concatenate([f[:64], pack(jnp.where(jj[:64] >= 64, x, -y))], axis=0)
                for f, x, y in zip(fulls, small, lows)
            ]
            for c in range(count):
                for h in range(2):
                    x_ref[g, c, h] = inverses[2 * c + h]
            return carry

        lax.fori_loop(0, groups, prepare, 0)

        @pl.when(s == 0)
        def _():
            for r in range(1, n_sol):
                state_copy(r, lax.rem(my_sol + n_sol - r, n_sol)).wait_recv()

        for g in range(groups):
            for h in range(2):
                s_ref[g, :, h * C : (h + 1) * C] = every_ref[owner_ref[s], 2 * g + h].astype(F32)

        def advance(c, carry):
            span = pl.ds(pl.multiple_of(c * C, C), C)
            place = c * C + lax.broadcasted_iota(jnp.int32, (C, 1), 0)
            live = place < ends_ref[s, 1]
            row = lax.broadcasted_iota(jnp.int32, (8, C), 0)
            lane = c * C + lax.broadcasted_iota(jnp.int32, (8, C), 1)
            pick = jnp.where(
                ((row == 0) & (lane == ends_ref[s, 0] - 1)) | ((row == 1) & (lane == ends_ref[s, 1] - 1)),
                1.0, 0.0,
            ).astype(BF16)
            for g in range(groups):
                state = s_ref[g]
                sh, sl = split(state)
                kqp = kq_ref[g, c]
                reads = dot(kqp, jnp.concatenate([sh, sh], axis=0)) + dot(kqp[:, :C], sl)
                rows = rows_ref[g, c]
                cols = jnp.transpose(rows)
                tails, keeps = [], []
                for h in range(2):
                    part = slice(h * C, (h + 1) * C)
                    cum = cols[:, h : h + 1]
                    grown = jnp.exp(cum)
                    last = rows[h : h + 1, C - 1 : C]
                    right = vb_ref[g, c, :, part] - (cols[:, 2 + h : 3 + h] * grown) * reads[:C, part]
                    fresh = packed_dot(x_ref[g, c, h], pack_right(right))
                    core = grown * reads[C:, part] + packed_dot(score_ref[g, c, h], pack_right(fresh))
                    tails.append(fresh * jnp.exp(last - cum))
                    keeps.append(jnp.exp(last) * state[:, part])
                    scale = lax.rsqrt(jnp.mean(core * core, axis=-1, keepdims=True) + 1e-06)
                    chan = pl.ds((2 * g + h) * C, C)
                    gate = gate_ref[s, span, chan].astype(F32)
                    out = core * scale * gain_ref[...] * silu(gate)
                    hid = jnp.where(live, out, 0.0).astype(BF16)
                    for d in range(per_chunk):
                        hid_ref[c * per_chunk + d, s, :, chan] = hid[d * share : (d + 1) * share]
                    chosen = dot(pick, hid)
                    old = jnp.where(c == 0, 0.0, sel_ref[s, :, chan])
                    sel_ref[s, :, chan] = old + chosen
                fresh = jnp.concatenate(tails, axis=1)
                fh, fl = split(fresh)
                ktp = kt_ref[g, c]
                s_ref[g] = (
                    jnp.concatenate(keeps, axis=1)
                    + dot(ktp, jnp.concatenate([fh, fh], axis=0))
                    + dot(ktp[:, :C], fl)
                )
            for d in range(per_chunk):
                to = c * per_chunk + d

                @pl.when(to == me)
                def _():
                    hidden_local(s).start()

                @pl.when(to != me)
                def _():
                    hidden_copy(s, to, me).start()

            return carry

        lax.fori_loop(0, count, advance, 0)
        logit = jnp.sum(sel_ref[s] * probe_ref[me], axis=-1, keepdims=True)
        part_ref[me, s] = jnp.broadcast_to(logit, (8, C))
        return carry

    lax.fori_loop(0, sols, one_solution, 0)

    for r in range(1, shares):
        part_copy(r, me).start()
    for r in range(1, shares):
        part_copy(r, me).wait_send()
        part_copy(r, lax.rem(me + shares - r, shares)).wait_recv()
    total = part_ref[0]
    for other in range(1, shares):
        total = total + part_ref[other]
    logit_ref[...] = total
    for r in range(1, n_sol):
        state_copy(r, my_sol).wait_send()
    for s in range(sols):
        hidden_local(s).wait()
        for r in range(1, shares):
            hidden_copy(s, lax.rem(me + r, shares), me).wait_send()
            other = lax.rem(me + shares - r, shares)
            hidden_copy(s, other, other).wait_recv()


def run_layer(ends, owner, qk, v, gate, decay, beta, rate, bias, tqk, tv, own, gain, probe):
    sols, length, width = v.shape
    groups = width // C // 2
    count = length // C
    shares = lax.axis_size(("head", "sub"))
    n_sol = lax.axis_size("sol")
    smem = pl.BlockSpec(memory_space=pltpu.SMEM)
    vmem = pl.BlockSpec(memory_space=pltpu.VMEM)
    return pl.pallas_call(
        kernel,
        out_shape=(
            jax.ShapeDtypeStruct((sols, length // shares, shares * width), BF16),
            jax.ShapeDtypeStruct((sols, 8, C), F32),
        ),
        in_specs=[smem] * 2 + [vmem] * 5 + [smem] * 2 + [vmem] * 5,
        out_specs=(pl.BlockSpec(memory_space=pl.ANY), vmem),
        scratch_shapes=[
            pltpu.VMEM((shares, sols, length // shares, width), BF16),
            pltpu.VMEM((sols, 8, width), F32),
            pltpu.VMEM((groups, count, 8, C), F32),
            pltpu.VMEM((groups, count, 2 * C, 2 * C), BF16),
            pltpu.VMEM((groups, count, C, 2 * C), BF16),
            pltpu.VMEM((groups, count, 2, C, 2 * C), BF16),
            pltpu.VMEM((groups, count, 2, C, 2 * C), BF16),
            pltpu.VMEM((groups, count, C, 2 * C), F32),
            pltpu.VMEM((groups, C, 2 * C), F32),
            pltpu.VMEM((n_sol * own.shape[0],) + own.shape[1:], BF16),
            pltpu.VMEM((shares, sols, 8, C), F32),
            pltpu.VMEM((8, C, 2 * C), BF16),
            pltpu.SemaphoreType.DMA((n_sol - 1,)),
            pltpu.SemaphoreType.DMA((n_sol - 1,)),
            pltpu.SemaphoreType.DMA((sols, shares)),
            pltpu.SemaphoreType.DMA((sols, shares)),
            pltpu.SemaphoreType.DMA((shares - 1,)),
            pltpu.SemaphoreType.DMA((shares - 1,)),
            pltpu.SemaphoreType.DMA((sols,)),
        ],
        compiler_params=pltpu.CompilerParams(vmem_limit_bytes=56 * 1024 * 1024, collective_id=0, has_side_effects=True),
        name="delta_layer",
    )(ends, owner, qk, v, gate, decay, beta, rate, bias, tqk, tv, own, gain, probe)


def on_device(
    query_key, values_in, gate_in, decay_in, beta_in, decay_rate, decay_bias, conv_qk, conv_v,
    prompt_states, prompt_of, step_ends, norm_gain, probe,
):
    sols, length, _, key_width = query_key.shape
    width = values_in.shape[2]
    shares = lax.axis_size(("head", "sub"))
    hidden, logits = run_layer(
        step_ends, prompt_of,
        query_key.reshape(sols, length, 2 * key_width),
        values_in, gate_in, decay_in, beta_in, decay_rate, decay_bias,
        conv_qk, conv_v, prompt_states, norm_gain[None, :],
        probe.astype(F32).reshape(shares, 1, width),
    )
    return hidden, logits[:, :2, 0]


def solution(mesh):
    return jax.shard_map(
        on_device,
        mesh=mesh,
        in_specs=(
            P(("groups", "sol"), None, None, ("head", "sub")),
            P(("groups", "sol"), None, ("head", "sub")),
            P(("groups", "sol"), None, ("head", "sub")),
            P(("groups", "sol"), ("head", "sub"), None),
            P(("groups", "sol"), ("head", "sub"), None),
            P(("head", "sub")),
            P(("head", "sub")),
            P(None, None, ("head", "sub")),
            P(None, ("head", "sub")),
            P(("groups", "sol"), ("head", "sub"), None, None),
            P(("groups", "sol")),
            P(("groups", "sol"), None),
            P(),
            P(),
        ),
        out_specs=(P(("groups", "sol"), ("head", "sub"), None), P(("groups", "sol"), None)),
        check_vma=False,
    )
```

```python
import jax
import jax.numpy as jnp
from jax import lax
from jax.experimental import pallas as pl
from jax.experimental.pallas import tpu as pltpu
from jax.sharding import PartitionSpec as P

C = 128
F32 = jnp.float32
BF16 = jnp.bfloat16
MESH = pl.DeviceIdType.MESH


def dot(a, b):
    return lax.dot_general(a, b, (((1,), (0,)), ((), ())), preferred_element_type=F32)


def split(x):
    high = x.astype(BF16)
    return high, (x - high.astype(F32)).astype(BF16)


def pack(x):
    return jnp.concatenate(split(x), axis=1)


def pack_right(x):
    row = pack(x)
    return jnp.concatenate([row, row], axis=0)


def packed_dot(left, right):
    both = dot(left, right)
    return both[:, :C] + both[:, C:]


def stacked_dot(left, right):
    rows = left.shape[0]
    both = dot(jnp.concatenate([left[:, :C], left[:, C:]], axis=0), right)
    both = both[:rows] + both[rows:]
    return both[:, :C] + both[:, C:]


def silu(x):
    return x / (1.0 + jnp.exp(-x))


def conv_silu(x, taps):
    rows = lax.broadcasted_iota(jnp.int32, x.shape, 0)
    total = x * taps[3:4]
    for back in range(1, 4):
        moved = jnp.where(rows >= back, pltpu.roll(x, back, 0), 0.0)
        total = total + moved * taps[3 - back : 4 - back]
    return silu(total)


def unit(x):
    return x * lax.rsqrt(jnp.sum(x * x, axis=-1, keepdims=True) + 1e-06)


def kernel(
    ends_ref, owner_ref, qk_ref, v_ref, gate_ref, decay_ref, beta_ref, rate_ref, bias_ref, tqk_ref, tv_ref,
    own_ref, gain_ref, probe_ref, out_ref, logit_ref, hid_ref, sel_ref, rows_ref, kq_ref, kt_ref, x_ref,
    score_ref, vb_ref, s_ref, every_ref, part_ref, mask_ref, st_send, st_recv, hid_send, hid_recv, lg_send, lg_recv, local_sem,
):
    sols, length, width = v_ref.shape
    n_sol, n_sub = lax.axis_size("sol"), lax.axis_size("sub")
    shares = lax.axis_size("head") * n_sub
    share = length // shares
    per_chunk = C // share
    prompts = own_ref.shape[0]
    my_sol = lax.axis_index("sol")
    me = lax.axis_index("head") * n_sub + lax.axis_index("sub")

    def mate(index):
        return {"head": index // n_sub, "sub": index % n_sub}

    barrier = pltpu.get_barrier_semaphore()
    for r in range(1, n_sol):
        pl.semaphore_signal(barrier, 1, device_id={"sol": lax.rem(my_sol + r, n_sol)}, device_id_type=MESH)
    for r in range(1, shares):
        pl.semaphore_signal(barrier, 1, device_id=mate(lax.rem(me + r, shares)), device_id_type=MESH)
    pl.semaphore_wait(barrier, n_sol + shares - 2)

    def state_copy(r, slot):
        return pltpu.make_async_remote_copy(
            src_ref=own_ref, dst_ref=every_ref.at[pl.ds(slot * prompts, prompts)],
            send_sem=st_send.at[r - 1], recv_sem=st_recv.at[r - 1],
            device_id={"sol": lax.rem(my_sol + r, n_sol)}, device_id_type=MESH,
        )

    def hidden_copy(s, to, source):
        return pltpu.make_async_remote_copy(
            src_ref=hid_ref.at[to, s],
            dst_ref=out_ref.at[s, :, pl.ds(pl.multiple_of(source * width, width), width)],
            send_sem=hid_send.at[s, to], recv_sem=hid_recv.at[s, source],
            device_id=mate(to), device_id_type=MESH,
        )

    def hidden_local(s):
        return pltpu.make_async_copy(
            hid_ref.at[me, s], out_ref.at[s, :, pl.ds(pl.multiple_of(me * width, width), width)],
            local_sem.at[s],
        )

    def part_copy(r, slot):
        return pltpu.make_async_remote_copy(
            src_ref=part_ref.at[slot], dst_ref=part_ref.at[slot],
            send_sem=lg_send.at[r - 1], recv_sem=lg_recv.at[r - 1],
            device_id=mate(lax.rem(me + r, shares)), device_id_type=MESH,
        )

    for r in range(1, n_sol):
        state_copy(r, my_sol).start()
    every_ref[pl.ds(my_sol * prompts, prompts)] = own_ref[...]
    heads = width // C
    groups = heads // 2
    count = length // C
    ii = lax.broadcasted_iota(jnp.int32, (C, C), 0)
    jj = lax.broadcasted_iota(jnp.int32, (C, C), 1)
    ones = jnp.where(ii <= jj, 1.0, 0.0).astype(F32)
    far = ii ^ jj
    for at, (least, most) in enumerate(((2, 4), (4, 8), (8, 16), (16, 32), (32, 64), (64, 128), (0, 32), (0, 64))):
        mask = jnp.where((far >= least) & (far < most), 1.0, 0.0).astype(BF16)
        mask_ref[at] = jnp.concatenate([mask, mask], axis=1)
    head = lax.broadcasted_iota(jnp.int32, (heads, 1), 0)
    rate_col = jnp.zeros((heads, 1), F32)
    bias_col = jnp.zeros((heads, 1), F32)
    for h in range(heads):
        rate_col = jnp.where(head == h, rate_ref[h], rate_col)
        bias_col = jnp.where(head == h, bias_ref[h], bias_col)

    def one_solution(s, carry):
        log_decay = -rate_col * jax.nn.softplus(decay_ref[s] + bias_col)
        beta = jax.nn.sigmoid(beta_ref[s])
        for c in range(count):
            cols = slice(c * C, (c + 1) * C)
            cum = lax.dot_general(
                log_decay[:, cols], ones, (((1,), (0,)), ((), ())),
                precision=lax.Precision.HIGHEST, preferred_element_type=F32,
            )
            for g in range(groups):
                pair = slice(2 * g, 2 * g + 2)
                rows_ref[g, c] = jnp.concatenate(
                    [cum[pair], beta[pair, cols], jnp.zeros((4, C), F32)], axis=0
                )

        def prepare(g, carry):
            at = pl.ds(pl.multiple_of(g * C, C), C)
            at2 = pl.ds(pl.multiple_of(width // 2 + g * C, C), C)
            q = unit(conv_silu(qk_ref[s, :, at].astype(F32), tqk_ref[:, 0, at])) * C ** (-0.5)
            k = unit(conv_silu(qk_ref[s, :, at2].astype(F32), tqk_ref[:, 1, at]))
            atv = pl.ds(pl.multiple_of(g * 2 * C, 2 * C), 2 * C)
            v = conv_silu(v_ref[s, :, atv].astype(F32), tv_ref[:, atv])
            systems = []
            for c in range(count):
                span = slice(c * C, (c + 1) * C)
                kt = jnp.transpose(k[span])
                kth, ktl = split(kt)
                ktp = jnp.concatenate([kth, ktl], axis=1)
                kt_ref[g, c] = ktp
                kqp = jnp.concatenate([pack(k[span]), pack(q[span])], axis=0)
                kq_ref[g, c] = kqp
                gram = packed_dot(kqp, jnp.concatenate([ktp, ktp], axis=0))
                rows = rows_ref[g, c]
                cols = jnp.transpose(rows)
                for h in range(2):
                    spread = cols[:, h : h + 1] - rows[h : h + 1, :]
                    weights = jnp.exp(jnp.where(ii >= jj, spread, -1e30))
                    rate = cols[:, 2 + h : 3 + h]
                    score_ref[g, c, h] = pack(gram[C:] * weights)
                    systems.append(jnp.where(ii > jj, rate * gram[:C] * weights, 0.0))
                    vb_ref[g, c, :, h * C : (h + 1) * C] = rate * v[span, h * C : (h + 1) * C]
            parts = [pack(m) for m in systems]
            wide = [jnp.where((ii ^ jj) == 1, m, 0.0) for m in systems]
            eye = jnp.where((ii[:32] ^ (jj[:32] & 31)) == 0, 1.0, 0.0)
            small = [eye - (m[:32] + m[32:64] + m[64:96] + m[96:]) for m in wide]

            def tile(p, at):
                return jnp.concatenate([p] * (C // p.shape[0]), axis=0) * mask_ref[at]

            def near(p, at):
                return p * mask_ref[at]

            for level in range(4):
                packs = [pack(x) for x in small]
                mids = [stacked_dot(p, near(m, level)) for p, m in zip(packs, parts)]
                small = [x - stacked_dot(pack(y), tile(p, 6)) for x, y, p in zip(small, mids, packs)]
            half = lax.broadcasted_iota(jnp.int32, (64, C), 0) ^ lax.broadcasted_iota(jnp.int32, (64, C), 1)
            small = [jnp.where((half & 32) == 0, jnp.concatenate([x, x], axis=0), 0.0) for x in small]
            packs = [pack(x) for x in small]
            mids = [stacked_dot(p, near(m, 4)) for p, m in zip(packs, parts)]
            small = [x - stacked_dot(pack(y), tile(p, 7)) for x, y, p in zip(small, mids, packs)]
            packs = [pack(x) for x in small]
            fulls = [jnp.concatenate([p, p], axis=0) * mask_ref[7] for p in packs]
            mids = [stacked_dot(f[64:], near(m, 5)) for f, m in zip(fulls, parts)]
            lows = [stacked_dot(pack(y), f) for y, f in zip(mids, fulls)]
            inverses = [
                jnp.concatenate([f[:64], pack(jnp.where(jj[:64] >= 64, x, -y))], axis=0)
                for f, x, y in zip(fulls, small, lows)
            ]
            for c in range(count):
                for h in range(2):
                    x_ref[g, c, h] = inverses[2 * c + h]
            return carry

        lax.fori_loop(0, groups, prepare, 0)

        @pl.when(s == 0)
        def _():
            for r in range(1, n_sol):
                state_copy(r, lax.rem(my_sol + n_sol - r, n_sol)).wait_recv()

        for g in range(groups):
            for h in range(2):
                s_ref[g, :, h * C : (h + 1) * C] = every_ref[owner_ref[s], 2 * g + h].astype(F32)

        def advance(c, carry):
            span = pl.ds(pl.multiple_of(c * C, C), C)
            place = c * C + lax.broadcasted_iota(jnp.int32, (C, 1), 0)
            live = place < ends_ref[s, 1]
            row = lax.broadcasted_iota(jnp.int32, (8, C), 0)
            lane = c * C + lax.broadcasted_iota(jnp.int32, (8, C), 1)
            pick = jnp.where(
                ((row == 0) & (lane == ends_ref[s, 0] - 1)) | ((row == 1) & (lane == ends_ref[s, 1] - 1)),
                1.0, 0.0,
            ).astype(BF16)
            for g in range(groups):
                state = s_ref[g]
                sh, sl = split(state)
                kqp = kq_ref[g, c]
                reads = dot(kqp, jnp.concatenate([sh, sh], axis=0)) + dot(kqp[:, :C], sl)
                rows = rows_ref[g, c]
                cols = jnp.transpose(rows)
                tails, keeps = [], []
                for h in range(2):
                    part = slice(h * C, (h + 1) * C)
                    cum = cols[:, h : h + 1]
                    grown = jnp.exp(cum)
                    last = rows[h : h + 1, C - 1 : C]
                    right = vb_ref[g, c, :, part] - (cols[:, 2 + h : 3 + h] * grown) * reads[:C, part]
                    fresh = packed_dot(x_ref[g, c, h], pack_right(right))
                    core = grown * reads[C:, part] + packed_dot(score_ref[g, c, h], pack_right(fresh))
                    tails.append(fresh * jnp.exp(last - cum))
                    keeps.append(jnp.exp(last) * state[:, part])
                    scale = lax.rsqrt(jnp.mean(core * core, axis=-1, keepdims=True) + 1e-06)
                    chan = pl.ds((2 * g + h) * C, C)
                    gate = gate_ref[s, span, chan].astype(F32)
                    out = core * scale * gain_ref[...] * silu(gate)
                    hid = jnp.where(live, out, 0.0).astype(BF16)
                    for d in range(per_chunk):
                        hid_ref[c * per_chunk + d, s, :, chan] = hid[d * share : (d + 1) * share]
                    chosen = dot(pick, hid)
                    old = jnp.where(c == 0, 0.0, sel_ref[s, :, chan])
                    sel_ref[s, :, chan] = old + chosen
                fresh = jnp.concatenate(tails, axis=1)
                fh, fl = split(fresh)
                ktp = kt_ref[g, c]
                s_ref[g] = (
                    jnp.concatenate(keeps, axis=1)
                    + dot(ktp, jnp.concatenate([fh, fh], axis=0))
                    + dot(ktp[:, :C], fl)
                )
            for d in range(per_chunk):
                to = c * per_chunk + d

                @pl.when(to == me)
                def _():
                    hidden_local(s).start()

                @pl.when(to != me)
                def _():
                    hidden_copy(s, to, me).start()

            return carry

        lax.fori_loop(0, count, advance, 0)
        logit = jnp.sum(sel_ref[s] * probe_ref[me], axis=-1, keepdims=True)
        part_ref[me, s] = jnp.broadcast_to(logit, (8, C))
        return carry

    lax.fori_loop(0, sols, one_solution, 0)

    for r in range(1, shares):
        part_copy(r, me).start()
    for r in range(1, shares):
        part_copy(r, me).wait_send()
        part_copy(r, lax.rem(me + shares - r, shares)).wait_recv()
    total = part_ref[0]
    for other in range(1, shares):
        total = total + part_ref[other]
    logit_ref[...] = total
    for r in range(1, n_sol):
        state_copy(r, my_sol).wait_send()
    for s in range(sols):
        hidden_local(s).wait()
        for r in range(1, shares):
            hidden_copy(s, lax.rem(me + r, shares), me).wait_send()
            other = lax.rem(me + shares - r, shares)
            hidden_copy(s, other, other).wait_recv()


def run_layer(ends, owner, qk, v, gate, decay, beta, rate, bias, tqk, tv, own, gain, probe):
    sols, length, width = v.shape
    groups = width // C // 2
    count = length // C
    shares = lax.axis_size(("head", "sub"))
    n_sol = lax.axis_size("sol")
    smem = pl.BlockSpec(memory_space=pltpu.SMEM)
    vmem = pl.BlockSpec(memory_space=pltpu.VMEM)
    return pl.pallas_call(
        kernel,
        out_shape=(
            jax.ShapeDtypeStruct((sols, length // shares, shares * width), BF16),
            jax.ShapeDtypeStruct((sols, 8, C), F32),
        ),
        in_specs=[smem] * 2 + [vmem] * 5 + [smem] * 2 + [vmem] * 5,
        out_specs=(pl.BlockSpec(memory_space=pl.ANY), vmem),
        scratch_shapes=[
            pltpu.VMEM((shares, sols, length // shares, width), BF16),
            pltpu.VMEM((sols, 8, width), F32),
            pltpu.VMEM((groups, count, 8, C), F32),
            pltpu.VMEM((groups, count, 2 * C, 2 * C), BF16),
            pltpu.VMEM((groups, count, C, 2 * C), BF16),
            pltpu.VMEM((groups, count, 2, C, 2 * C), BF16),
            pltpu.VMEM((groups, count, 2, C, 2 * C), BF16),
            pltpu.VMEM((groups, count, C, 2 * C), F32),
            pltpu.VMEM((groups, C, 2 * C), F32),
            pltpu.VMEM((n_sol * own.shape[0],) + own.shape[1:], BF16),
            pltpu.VMEM((shares, sols, 8, C), F32),
            pltpu.VMEM((8, C, 2 * C), BF16),
            pltpu.SemaphoreType.DMA((n_sol - 1,)),
            pltpu.SemaphoreType.DMA((n_sol - 1,)),
            pltpu.SemaphoreType.DMA((sols, shares)),
            pltpu.SemaphoreType.DMA((sols, shares)),
            pltpu.SemaphoreType.DMA((shares - 1,)),
            pltpu.SemaphoreType.DMA((shares - 1,)),
            pltpu.SemaphoreType.DMA((sols,)),
        ],
        compiler_params=pltpu.CompilerParams(vmem_limit_bytes=56 * 1024 * 1024, collective_id=0, has_side_effects=True),
        name="delta_layer",
    )(ends, owner, qk, v, gate, decay, beta, rate, bias, tqk, tv, own, gain, probe)


def on_device(
    query_key, values_in, gate_in, decay_in, beta_in, decay_rate, decay_bias, conv_qk, conv_v,
    prompt_states, prompt_of, step_ends, norm_gain, probe,
):
    sols, length, _, key_width = query_key.shape
    width = values_in.shape[2]
    shares = lax.axis_size(("head", "sub"))
    hidden, logits = run_layer(
        step_ends, prompt_of,
        query_key.reshape(sols, length, 2 * key_width),
        values_in, gate_in, decay_in, beta_in, decay_rate, decay_bias,
        conv_qk, conv_v, prompt_states, norm_gain[None, :],
        probe.astype(F32).reshape(shares, 1, width),
    )
    return hidden, logits[:, :2, 0]


def solution(mesh):
    return jax.shard_map(
        on_device,
        mesh=mesh,
        in_specs=(
            P(("groups", "sol"), None, None, ("head", "sub")),
            P(("groups", "sol"), None, ("head", "sub")),
            P(("groups", "sol"), None, ("head", "sub")),
            P(("groups", "sol"), ("head", "sub"), None),
            P(("groups", "sol"), ("head", "sub"), None),
            P(("head", "sub")),
            P(("head", "sub")),
            P(None, None, ("head", "sub")),
            P(None, ("head", "sub")),
            P(("groups", "sol"), ("head", "sub"), None, None),
            P(("groups", "sol")),
            P(("groups", "sol"), None),
            P(),
            P(),
        ),
        out_specs=(P(("groups", "sol"), ("head", "sub"), None), P(("groups", "sol"), None)),
        check_vma=False,
    )
```

```python
import jax
import jax.numpy as jnp
from jax import lax
from jax.experimental import pallas as pl
from jax.experimental.pallas import tpu as pltpu
from jax.sharding import PartitionSpec as P

C = 128
F32 = jnp.float32
BF16 = jnp.bfloat16
MESH = pl.DeviceIdType.MESH


def dot(a, b):
    return lax.dot_general(a, b, (((1,), (0,)), ((), ())), preferred_element_type=F32)


def split(x):
    high = x.astype(BF16)
    return high, (x - high.astype(F32)).astype(BF16)


def pack(x):
    return jnp.concatenate(split(x), axis=1)


def pack_right(x):
    row = pack(x)
    return jnp.concatenate([row, row], axis=0)


def packed_dot(left, right):
    both = dot(left, right)
    return both[:, :C] + both[:, C:]


def stacked_dot(left, right):
    rows = left.shape[0]
    both = dot(jnp.concatenate([left[:, :C], left[:, C:]], axis=0), right)
    both = both[:rows] + both[rows:]
    return both[:, :C] + both[:, C:]


def silu(x):
    return x / (1.0 + jnp.exp(-x))


def conv_silu(x, taps):
    rows = lax.broadcasted_iota(jnp.int32, x.shape, 0)
    total = x * taps[3:4]
    for back in range(1, 4):
        moved = jnp.where(rows >= back, pltpu.roll(x, back, 0), 0.0)
        total = total + moved * taps[3 - back : 4 - back]
    return silu(total)


def unit(x):
    return x * lax.rsqrt(jnp.sum(x * x, axis=-1, keepdims=True) + 1e-06)


def kernel(
    ends_ref, owner_ref, qk_ref, v_ref, gate_ref, decay_ref, beta_ref, rate_ref, bias_ref, tqk_ref, tv_ref,
    own_ref, gain_ref, probe_ref, out_ref, logit_ref, hid_ref, sel_ref, rows_ref, kq_ref, kt_ref, x_ref,
    score_ref, vb_ref, s_ref, every_ref, part_ref, mask_ref, st_send, st_recv, hid_send, hid_recv, lg_send, lg_recv, local_sem,
):
    sols, length, width = v_ref.shape
    n_sol, n_sub = lax.axis_size("sol"), lax.axis_size("sub")
    shares = lax.axis_size("head") * n_sub
    share = length // shares
    per_chunk = C // share
    prompts = own_ref.shape[0]
    my_sol = lax.axis_index("sol")
    me = lax.axis_index("head") * n_sub + lax.axis_index("sub")

    def mate(index):
        return {"head": index // n_sub, "sub": index % n_sub}

    barrier = pltpu.get_barrier_semaphore()
    for r in range(1, n_sol):
        pl.semaphore_signal(barrier, 1, device_id={"sol": lax.rem(my_sol + r, n_sol)}, device_id_type=MESH)
    for r in range(1, shares):
        pl.semaphore_signal(barrier, 1, device_id=mate(lax.rem(me + r, shares)), device_id_type=MESH)
    pl.semaphore_wait(barrier, n_sol + shares - 2)

    def state_copy(r, slot):
        return pltpu.make_async_remote_copy(
            src_ref=own_ref, dst_ref=every_ref.at[pl.ds(slot * prompts, prompts)],
            send_sem=st_send.at[r - 1], recv_sem=st_recv.at[r - 1],
            device_id={"sol": lax.rem(my_sol + r, n_sol)}, device_id_type=MESH,
        )

    def hidden_copy(s, to, source):
        return pltpu.make_async_remote_copy(
            src_ref=hid_ref.at[to, s],
            dst_ref=out_ref.at[s, :, pl.ds(pl.multiple_of(source * width, width), width)],
            send_sem=hid_send.at[s, to], recv_sem=hid_recv.at[s, source],
            device_id=mate(to), device_id_type=MESH,
        )

    def hidden_local(s):
        return pltpu.make_async_copy(
            hid_ref.at[me, s], out_ref.at[s, :, pl.ds(pl.multiple_of(me * width, width), width)],
            local_sem.at[s],
        )

    def part_copy(r, slot):
        return pltpu.make_async_remote_copy(
            src_ref=part_ref.at[slot], dst_ref=part_ref.at[slot],
            send_sem=lg_send.at[r - 1], recv_sem=lg_recv.at[r - 1],
            device_id=mate(lax.rem(me + r, shares)), device_id_type=MESH,
        )

    for r in range(1, n_sol):
        state_copy(r, my_sol).start()
    every_ref[pl.ds(my_sol * prompts, prompts)] = own_ref[...]
    heads = width // C
    groups = heads // 2
    count = length // C
    ii = lax.broadcasted_iota(jnp.int32, (C, C), 0)
    jj = lax.broadcasted_iota(jnp.int32, (C, C), 1)
    ones = jnp.where(ii <= jj, 1.0, 0.0).astype(F32)
    far = ii ^ jj
    for at, (least, most) in enumerate(((2, 4), (4, 8), (8, 16), (16, 32), (32, 64), (64, 128), (0, 32), (0, 64))):
        mask = jnp.where((far >= least) & (far < most), 1.0, 0.0).astype(BF16)
        mask_ref[at] = jnp.concatenate([mask, mask], axis=1)
    head = lax.broadcasted_iota(jnp.int32, (heads, 1), 0)
    rate_col = jnp.zeros((heads, 1), F32)
    bias_col = jnp.zeros((heads, 1), F32)
    for h in range(heads):
        rate_col = jnp.where(head == h, rate_ref[h], rate_col)
        bias_col = jnp.where(head == h, bias_ref[h], bias_col)

    def one_solution(s, carry):
        log_decay = -rate_col * jax.nn.softplus(decay_ref[s] + bias_col)
        beta = jax.nn.sigmoid(beta_ref[s])
        for c in range(count):
            cols = slice(c * C, (c + 1) * C)
            cum = lax.dot_general(
                log_decay[:, cols], ones, (((1,), (0,)), ((), ())),
                precision=lax.Precision.HIGHEST, preferred_element_type=F32,
            )
            for g in range(groups):
                pair = slice(2 * g, 2 * g + 2)
                rows_ref[g, c] = jnp.concatenate(
                    [cum[pair], beta[pair, cols], jnp.zeros((4, C), F32)], axis=0
                )

        def prepare(g, carry):
            at = pl.ds(pl.multiple_of(g * C, C), C)
            at2 = pl.ds(pl.multiple_of(width // 2 + g * C, C), C)
            q = unit(conv_silu(qk_ref[s, :, at].astype(F32), tqk_ref[:, 0, at])) * C ** (-0.5)
            k = unit(conv_silu(qk_ref[s, :, at2].astype(F32), tqk_ref[:, 1, at]))
            atv = pl.ds(pl.multiple_of(g * 2 * C, 2 * C), 2 * C)
            v = conv_silu(v_ref[s, :, atv].astype(F32), tv_ref[:, atv])
            systems = []
            for c in range(count):
                span = slice(c * C, (c + 1) * C)
                kt = jnp.transpose(k[span])
                kth, ktl = split(kt)
                ktp = jnp.concatenate([kth, ktl], axis=1)
                kt_ref[g, c] = ktp
                kqp = jnp.concatenate([pack(k[span]), pack(q[span])], axis=0)
                kq_ref[g, c] = kqp
                gram = packed_dot(kqp, jnp.concatenate([ktp, ktp], axis=0))
                rows = rows_ref[g, c]
                cols = jnp.transpose(rows)
                for h in range(2):
                    spread = cols[:, h : h + 1] - rows[h : h + 1, :]
                    weights = jnp.exp(jnp.where(ii >= jj, spread, -1e30))
                    rate = cols[:, 2 + h : 3 + h]
                    score_ref[g, c, h] = pack(gram[C:] * weights)
                    systems.append(jnp.where(ii > jj, rate * gram[:C] * weights, 0.0))
                    vb_ref[g, c, :, h * C : (h + 1) * C] = rate * v[span, h * C : (h + 1) * C]
            parts = [pack(m) for m in systems]
            wide = [jnp.where((ii ^ jj) == 1, m, 0.0) for m in systems]
            eye = jnp.where((ii[:32] ^ (jj[:32] & 31)) == 0, 1.0, 0.0)
            small = [eye - (m[:32] + m[32:64] + m[64:96] + m[96:]) for m in wide]

            def tile(p, at):
                return jnp.concatenate([p] * (C // p.shape[0]), axis=0) * mask_ref[at]

            def near(p, at):
                return p * mask_ref[at]

            for level in range(4):
                packs = [pack(x) for x in small]
                mids = [stacked_dot(p, near(m, level)) for p, m in zip(packs, parts)]
                small = [x - stacked_dot(pack(y), tile(p, 6)) for x, y, p in zip(small, mids, packs)]
            half = lax.broadcasted_iota(jnp.int32, (64, C), 0) ^ lax.broadcasted_iota(jnp.int32, (64, C), 1)
            small = [jnp.where((half & 32) == 0, jnp.concatenate([x, x], axis=0), 0.0) for x in small]
            packs = [pack(x) for x in small]
            mids = [stacked_dot(p, near(m, 4)) for p, m in zip(packs, parts)]
            small = [x - stacked_dot(pack(y), tile(p, 7)) for x, y, p in zip(small, mids, packs)]
            packs = [pack(x) for x in small]
            fulls = [jnp.concatenate([p, p], axis=0) * mask_ref[7] for p in packs]
            mids = [stacked_dot(f[64:], near(m, 5)) for f, m in zip(fulls, parts)]
            lows = [stacked_dot(pack(y), f) for y, f in zip(mids, fulls)]
            inverses = [
                jnp.concatenate([f[:64], pack(jnp.where(jj[:64] >= 64, x, -y))], axis=0)
                for f, x, y in zip(fulls, small, lows)
            ]
            for c in range(count):
                for h in range(2):
                    x_ref[g, c, h] = inverses[2 * c + h]
            return carry

        lax.fori_loop(0, groups, prepare, 0, unroll=min(2, groups))

        @pl.when(s == 0)
        def _():
            for r in range(1, n_sol):
                state_copy(r, lax.rem(my_sol + n_sol - r, n_sol)).wait_recv()

        for g in range(groups):
            for h in range(2):
                s_ref[g, :, h * C : (h + 1) * C] = every_ref[owner_ref[s], 2 * g + h].astype(F32)

        def advance(c, carry):
            span = pl.ds(pl.multiple_of(c * C, C), C)
            place = c * C + lax.broadcasted_iota(jnp.int32, (C, 1), 0)
            live = place < ends_ref[s, 1]
            row = lax.broadcasted_iota(jnp.int32, (8, C), 0)
            lane = c * C + lax.broadcasted_iota(jnp.int32, (8, C), 1)
            pick = jnp.where(
                ((row == 0) & (lane == ends_ref[s, 0] - 1)) | ((row == 1) & (lane == ends_ref[s, 1] - 1)),
                1.0, 0.0,
            ).astype(BF16)
            for g in range(groups):
                state = s_ref[g]
                sh, sl = split(state)
                kqp = kq_ref[g, c]
                reads = dot(kqp, jnp.concatenate([sh, sh], axis=0)) + dot(kqp[:, :C], sl)
                rows = rows_ref[g, c]
                cols = jnp.transpose(rows)
                tails, keeps = [], []
                for h in range(2):
                    part = slice(h * C, (h + 1) * C)
                    cum = cols[:, h : h + 1]
                    grown = jnp.exp(cum)
                    last = rows[h : h + 1, C - 1 : C]
                    right = vb_ref[g, c, :, part] - (cols[:, 2 + h : 3 + h] * grown) * reads[:C, part]
                    fresh = packed_dot(x_ref[g, c, h], pack_right(right))
                    core = grown * reads[C:, part] + packed_dot(score_ref[g, c, h], pack_right(fresh))
                    tails.append(fresh * jnp.exp(last - cum))
                    keeps.append(jnp.exp(last) * state[:, part])
                    scale = lax.rsqrt(jnp.mean(core * core, axis=-1, keepdims=True) + 1e-06)
                    chan = pl.ds((2 * g + h) * C, C)
                    gate = gate_ref[s, span, chan].astype(F32)
                    out = core * scale * gain_ref[...] * silu(gate)
                    hid = jnp.where(live, out, 0.0).astype(BF16)
                    for d in range(per_chunk):
                        hid_ref[c * per_chunk + d, s, :, chan] = hid[d * share : (d + 1) * share]
                    chosen = dot(pick, hid)
                    old = jnp.where(c == 0, 0.0, sel_ref[s, :, chan])
                    sel_ref[s, :, chan] = old + chosen
                fresh = jnp.concatenate(tails, axis=1)
                fh, fl = split(fresh)
                ktp = kt_ref[g, c]
                s_ref[g] = (
                    jnp.concatenate(keeps, axis=1)
                    + dot(ktp, jnp.concatenate([fh, fh], axis=0))
                    + dot(ktp[:, :C], fl)
                )
            for d in range(per_chunk):
                to = c * per_chunk + d

                @pl.when(to == me)
                def _():
                    hidden_local(s).start()

                @pl.when(to != me)
                def _():
                    hidden_copy(s, to, me).start()

            return carry

        lax.fori_loop(0, count, advance, 0)
        logit = jnp.sum(sel_ref[s] * probe_ref[me], axis=-1, keepdims=True)
        part_ref[me, s] = jnp.broadcast_to(logit, (8, C))
        return carry

    lax.fori_loop(0, sols, one_solution, 0)

    for r in range(1, shares):
        part_copy(r, me).start()
    for r in range(1, shares):
        part_copy(r, me).wait_send()
        part_copy(r, lax.rem(me + shares - r, shares)).wait_recv()
    total = part_ref[0]
    for other in range(1, shares):
        total = total + part_ref[other]
    logit_ref[...] = total
    for r in range(1, n_sol):
        state_copy(r, my_sol).wait_send()
    for s in range(sols):
        hidden_local(s).wait()
        for r in range(1, shares):
            hidden_copy(s, lax.rem(me + r, shares), me).wait_send()
            other = lax.rem(me + shares - r, shares)
            hidden_copy(s, other, other).wait_recv()


def run_layer(ends, owner, qk, v, gate, decay, beta, rate, bias, tqk, tv, own, gain, probe):
    sols, length, width = v.shape
    groups = width // C // 2
    count = length // C
    shares = lax.axis_size(("head", "sub"))
    n_sol = lax.axis_size("sol")
    smem = pl.BlockSpec(memory_space=pltpu.SMEM)
    vmem = pl.BlockSpec(memory_space=pltpu.VMEM)
    return pl.pallas_call(
        kernel,
        out_shape=(
            jax.ShapeDtypeStruct((sols, length // shares, shares * width), BF16),
            jax.ShapeDtypeStruct((sols, 8, C), F32),
        ),
        in_specs=[smem] * 2 + [vmem] * 5 + [smem] * 2 + [vmem] * 5,
        out_specs=(pl.BlockSpec(memory_space=pl.ANY), vmem),
        scratch_shapes=[
            pltpu.VMEM((shares, sols, length // shares, width), BF16),
            pltpu.VMEM((sols, 8, width), F32),
            pltpu.VMEM((groups, count, 8, C), F32),
            pltpu.VMEM((groups, count, 2 * C, 2 * C), BF16),
            pltpu.VMEM((groups, count, C, 2 * C), BF16),
            pltpu.VMEM((groups, count, 2, C, 2 * C), BF16),
            pltpu.VMEM((groups, count, 2, C, 2 * C), BF16),
            pltpu.VMEM((groups, count, C, 2 * C), F32),
            pltpu.VMEM((groups, C, 2 * C), F32),
            pltpu.VMEM((n_sol * own.shape[0],) + own.shape[1:], BF16),
            pltpu.VMEM((shares, sols, 8, C), F32),
            pltpu.VMEM((8, C, 2 * C), BF16),
            pltpu.SemaphoreType.DMA((n_sol - 1,)),
            pltpu.SemaphoreType.DMA((n_sol - 1,)),
            pltpu.SemaphoreType.DMA((sols, shares)),
            pltpu.SemaphoreType.DMA((sols, shares)),
            pltpu.SemaphoreType.DMA((shares - 1,)),
            pltpu.SemaphoreType.DMA((shares - 1,)),
            pltpu.SemaphoreType.DMA((sols,)),
        ],
        compiler_params=pltpu.CompilerParams(vmem_limit_bytes=56 * 1024 * 1024, collective_id=0, has_side_effects=True),
        name="delta_layer",
    )(ends, owner, qk, v, gate, decay, beta, rate, bias, tqk, tv, own, gain, probe)


def on_device(
    query_key, values_in, gate_in, decay_in, beta_in, decay_rate, decay_bias, conv_qk, conv_v,
    prompt_states, prompt_of, step_ends, norm_gain, probe,
):
    sols, length, _, key_width = query_key.shape
    width = values_in.shape[2]
    shares = lax.axis_size(("head", "sub"))
    hidden, logits = run_layer(
        step_ends, prompt_of,
        query_key.reshape(sols, length, 2 * key_width),
        values_in, gate_in, decay_in, beta_in, decay_rate, decay_bias,
        conv_qk, conv_v, prompt_states, norm_gain[None, :],
        probe.astype(F32).reshape(shares, 1, width),
    )
    return hidden, logits[:, :2, 0]


def solution(mesh):
    return jax.shard_map(
        on_device,
        mesh=mesh,
        in_specs=(
            P(("groups", "sol"), None, None, ("head", "sub")),
            P(("groups", "sol"), None, ("head", "sub")),
            P(("groups", "sol"), None, ("head", "sub")),
            P(("groups", "sol"), ("head", "sub"), None),
            P(("groups", "sol"), ("head", "sub"), None),
            P(("head", "sub")),
            P(("head", "sub")),
            P(None, None, ("head", "sub")),
            P(None, ("head", "sub")),
            P(("groups", "sol"), ("head", "sub"), None, None),
            P(("groups", "sol")),
            P(("groups", "sol"), None),
            P(),
            P(),
        ),
        out_specs=(P(("groups", "sol"), ("head", "sub"), None), P(("groups", "sol"), None)),
        check_vma=False,
    )
```
